512 devices in a mesh: dp: 8 (over x, core), context: 16 (over y_lo, z), tensor: 4 (over y_hi).
Axes of the slice: x: 4, y: 8 (y_hi: 4, y_lo: 2; y = y_hi * 2 + y_lo), z: 8, core: 2. Of those that a mesh axis runs over, the one named last changes fastest.
Arguments:
- staying_cache: bfloat16 [16, 32, 256, 576], P('context', 'dp'), parts along dimension 1, may hold values from -6 to 6
- leaving_cache: bfloat16 [16, 32, 256, 576], P('context', 'dp'), parts along dimension 1, may hold values from -6 to 6
- lengths: int32 [32], P('dp'), parts along dimension 0, may hold values from 4096 to 8190, as said below
- pairing: int32 [32, 16], P('dp'), parts along dimension 0, may hold values from 0 to 15, as said below
- new_entries: bfloat16 [32, 2, 576], P('dp'), parts along dimension 0, may hold values from -6 to 6
- queries: bfloat16 [32, 2, 64, 576], P('dp', None, 'tensor'), parts along dimension 0, may hold values from -40 to 40
- w_value: bfloat16 [64, 512, 128], P('tensor', 'context'), may hold values from -2.390625 to 2.390625
- w_out: bfloat16 [8192, 7168], P('tensor', 'context'), may hold values from -0.0625 to 0.0625
Outputs:
- new_cache: bfloat16 [16, 32, 512, 576], P('context', 'dp'), parts along dimension 1
- attn_out: bfloat16 [32, 2, 7168], P('dp', None, ('context', 'tensor')), parts along dimension 0
The draws below stay inside these ranges and needn't reach their ends.
There are 8 independent parts, one for each index of `dp`. The reference program is written for one: setup_inputs(seed, part) draws one part's arguments, and reference() takes and returns one part's arrays. A program takes and returns all parts, laid end to end along the dimension named above; an argument that names none is the same for every part. Nothing has to cross between parts.
Inputs may be any that keep to these rules, and one draw needn't show every extreme that they name: pairing[b, j] = (j + m_b) mod 16 for one offset m_b of each request b, the same for every j. `lengths`: every draw has a request of length 8190.
All inputs are finite; a program needn't handle non-finite values.
Results may differ from the reference program's by a relative error of at most 0.015.
Values may be sent and summed in bfloat16 or wider, within the bound.
No kernel may reach another device: no remote copies, remote signals or barrier semaphores. Data moves between devices by JAX's collectives and lax.ppermute only.
A program may use at most 128 MiB of HBM per device.

```python
import math
import jax
import jax.numpy as jnp

D = 7168
HEADS = 64
LATENT = 512
ROPE = 64
VHEAD = 128
STEPS = 2
REQ = 4
SLICE = 256
MEMBERS = 16


def entry_values(key):
    return jnp.clip(jax.random.normal(key, (REQ, STEPS, LATENT + ROPE), jnp.float32), -6.0, 6.0)


def draw_new_entries(key, part):
    shared = entry_values(key)
    return shared.astype(jnp.bfloat16)


def draw_queries(key, part):
    shared = entry_values(key)
    key = jax.random.fold_in(key, 5)
    strength_key, jitter_key = jax.random.split(key)
    shape = (REQ, STEPS, HEADS, LATENT + ROPE)
    strength = jnp.exp(jax.random.uniform(strength_key, (1, 1, HEADS, 1), jnp.float32, math.log(0.18), math.log(0.3)))
    jitter = jnp.clip(jax.random.normal(jitter_key, shape, jnp.float32), -4.0, 4.0)
    return (strength * shared[:, :, None, :] + jitter).astype(jnp.bfloat16)


def draw_lengths(key, part):
    key = jax.random.fold_in(key, 11)
    length_key, ranking_key = jax.random.split(key)
    capacity = 2 * MEMBERS * SLICE
    picked = jax.random.randint(length_key, (REQ,), capacity // 2, capacity - 1)
    ranking = jax.random.permutation(ranking_key, REQ)
    picked = jnp.where(ranking == 0, capacity - 2, picked)
    return picked.astype(jnp.int32)


def draw_pairing(key, part):
    key = jax.random.fold_in(key, 13)
    offsets = jax.random.randint(key, (REQ, 1), 0, MEMBERS)
    return ((jnp.arange(MEMBERS, dtype=jnp.int32)[None, :] + offsets) % MEMBERS).astype(jnp.int32)


def level_of(own_key, shape, shards, least, high):
    gain, own = 1.0, jax.random.fold_in(own_key, 6)
    for axis_at, shards_of in shards:
        steps = jnp.exp(jax.random.uniform(jax.random.fold_in(own, axis_at), (shards_of,), jnp.float32, least / len(shards), high / len(shards)))
        gain = gain * jnp.repeat(steps, shape[axis_at] // shards_of).reshape([-1 if axis == axis_at else 1 for axis in range(len(shape))])
    return gain


def noise(rng, extent, spread, most, cuts=(), kind=jnp.bfloat16):
    values = jax.random.normal(rng, extent, jnp.float32) * spread
    if len(cuts) > 0:
        values = level_of(rng, extent, cuts, -0.22, 0.18) * values
    return jnp.clip(values, min=-most, max=most).astype(kind)


def setup_inputs(seed: int = 0, part: int = 0) -> dict:
    splits = jax.random.split(jax.random.key(seed), 9)
    part_keys = jax.random.split(jax.random.fold_in(splits[8], part), 9)
    staying_cache = noise(part_keys[0], (MEMBERS, REQ, SLICE, LATENT + ROPE), 1.0, 6.0, ((0, 16),))
    leaving_cache = noise(part_keys[1], (MEMBERS, REQ, SLICE, LATENT + ROPE), 1.0, 6.0, ((0, 16),))
    lengths = draw_lengths(jax.random.fold_in(jax.random.fold_in(splits[8], part), 71), part)
    pairing = draw_pairing(jax.random.fold_in(jax.random.fold_in(splits[8], part), 71), part)
    new_entries = draw_new_entries(jax.random.fold_in(jax.random.fold_in(splits[8], part), 71), part)
    queries = draw_queries(jax.random.fold_in(jax.random.fold_in(splits[8], part), 71), part)
    w_value = noise(splits[6], (HEADS, LATENT, VHEAD), 0.4, 2.390625, ((0, 4), (1, 16)))
    w_out = noise(splits[7], (HEADS * VHEAD, D), (HEADS * VHEAD) ** -0.5, 0.0625, ((0, 4), (1, 16)))
    return dict(staying_cache=staying_cache, leaving_cache=leaving_cache, lengths=lengths, pairing=pairing, new_entries=new_entries, queries=queries, w_value=w_value, w_out=w_out)


softmax_scale = 0.07216878364870322
large_negative = -1.0e30


def reference(staying_cache, leaving_cache, lengths, pairing, new_entries, queries, w_value, w_out):
    member_ids = jnp.arange(MEMBERS, dtype=jnp.int32)
    offsets = pairing[:, 0].astype(jnp.int32)
    sources = ((member_ids[:, None] - offsets[None, :]) % MEMBERS).astype(jnp.int32)
    request_ids = jnp.arange(REQ, dtype=jnp.int32)
    received = leaving_cache[sources, request_ids[None, :]]
    whole_cache = jnp.concatenate([staying_cache, received], axis=2)
    slot_ids = jnp.arange(SLICE, dtype=jnp.int32)
    own_positions = jnp.broadcast_to((member_ids[:, None] * SLICE + slot_ids[None, :])[:, None, :], (MEMBERS, REQ, SLICE))
    moved_positions = (MEMBERS + sources)[:, :, None] * SLICE + slot_ids[None, None, :]
    slot_positions = jnp.concatenate([own_positions, moved_positions], axis=2).astype(jnp.int32)
    for step_number in range(STEPS):
        target = slot_positions == (lengths + step_number)[None, :, None]
        whole_cache = jnp.where(target[..., None], new_entries[None, :, step_number, None, :], whole_cache)
    scores = jnp.einsum("bthw,nbjw->nbthj", queries.astype(jnp.float32), whole_cache.astype(jnp.float32)) * softmax_scale
    step_limit = lengths[:, None] + 1 + jnp.arange(STEPS, dtype=jnp.int32)[None, :]
    usable = slot_positions[:, :, None, None, :] < step_limit[None, :, :, None, None]
    masked = jnp.where(usable, scores, large_negative)
    member_peak = jnp.max(masked, axis=-1)
    weights = jnp.where(usable, jnp.exp(masked - member_peak[..., None]), 0.0).astype(jnp.bfloat16)
    latent_rows = whole_cache[..., :LATENT].astype(jnp.float32)
    numerators = jnp.einsum("nbthj,nbjl->nbthl", weights.astype(jnp.float32), latent_rows)
    totals = jnp.sum(weights.astype(jnp.float32), axis=-1)
    global_peak = jnp.max(member_peak, axis=0)
    rescale = jnp.exp(member_peak - global_peak[None])
    numerator = jnp.sum(rescale[..., None] * numerators, axis=0)
    total = jnp.sum(rescale * totals, axis=0)
    latent_out = (numerator / total[..., None]).astype(jnp.bfloat16)
    head_values = jnp.einsum("bthl,hlv->bthv", latent_out.astype(jnp.float32), w_value.astype(jnp.float32)).astype(jnp.bfloat16)
    flattened = head_values.reshape(REQ * STEPS, HEADS * VHEAD)
    attn_out = jnp.dot(flattened, w_out, preferred_element_type=jnp.float32).astype(jnp.bfloat16)
    return whole_cache, attn_out.reshape(REQ, STEPS, D)
```

```python
import jax
import jax.numpy as jnp
from jax import lax
from jax.experimental import pallas as pl
from jax.experimental.pallas import tpu as pltpu
from jax.sharding import PartitionSpec as P

REQ = 4
STEPS = 2
HEADS = 16
LATENT = 512
WIDTH = 576
SLICE = 256
MEMBERS = 16
TENSOR = 4
LANES = 128
CHUNK = WIDTH * SLICE // (MEMBERS * LANES)
VROWS = LATENT // MEMBERS
NROWS = 48
OUTC = 112

softmax_scale = 0.07216878364870322
large_negative = -1e30

f32 = jnp.float32
bf16 = jnp.bfloat16

VMEM = pl.BlockSpec(memory_space=pltpu.VMEM)
SMEM = pl.BlockSpec(memory_space=pltpu.SMEM)
ANY = pl.BlockSpec(memory_space=pl.ANY)


def nt_dot(a, b):
    return lax.dot_general(a, b, (((1,), (1,)), ((), ())), preferred_element_type=f32)


def with_new_entries(block, entries, length, member):
    first = (MEMBERS + member) * SLICE
    slot = lax.broadcasted_iota(jnp.int32, (STEPS, SLICE), 1)
    step = lax.broadcasted_iota(jnp.int32, (STEPS, SLICE), 0)
    hit = (slot + first == length + step).astype(f32)
    placed = lax.dot_general(
        entries, hit.astype(bf16), (((0,), (0,)), ((), ())), preferred_element_type=f32
    )
    taken = jnp.max(hit, axis=0, keepdims=True) > 0.5
    return jnp.where(taken, placed, block.astype(f32)).astype(bf16)


def pack_kernel(lengths, entries, leaving, w_value, out, block, sem):
    tensor = lax.axis_index("tensor")
    member = lax.axis_index("context")
    copy = pltpu.make_async_copy(leaving.at[tensor], block, sem)
    copy.start()
    out[:, 0:VROWS, :] = w_value[...]
    copy.wait()
    updated = with_new_entries(block[...], entries[tensor], lengths[tensor], member)
    for c in range(MEMBERS):
        row, lane = (c % 8) * CHUNK, (c // 8) * LANES
        out[c, VROWS : VROWS + CHUNK, :] = updated[row : row + CHUNK, lane : lane + LANES]


def attention_kernel(lengths, entries, queries, staying, leaving, out, cache, sem):
    member = lax.axis_index("context")
    copy = pltpu.make_async_copy(staying, cache.at[:, :, 0:SLICE], sem)
    copy.start()
    row = lax.broadcasted_iota(jnp.int32, (STEPS * HEADS, SLICE), 0)
    slot = lax.broadcasted_iota(jnp.int32, (STEPS * HEADS, SLICE), 1)
    step = (row >= HEADS).astype(jnp.int32)
    lane = lax.broadcasted_iota(jnp.int32, (STEPS * HEADS, LANES), 1)
    parts = []
    for b in range(REQ):
        q = queries[b]
        kept = staying[b]
        moved = with_new_entries(leaving[b], entries[b], lengths[b], member)
        limit = lengths[b] + 1 + step
        use_kept = slot + member * SLICE < limit
        use_moved = slot + (MEMBERS + member) * SLICE < limit
        kept_scores = jnp.dot(q, kept, preferred_element_type=f32) * softmax_scale
        moved_scores = jnp.dot(q, moved, preferred_element_type=f32) * softmax_scale
        kept_scores = jnp.where(use_kept, kept_scores, large_negative)
        moved_scores = jnp.where(use_moved, moved_scores, large_negative)
        peak = jnp.maximum(
            jnp.max(kept_scores, axis=1, keepdims=True),
            jnp.max(moved_scores, axis=1, keepdims=True),
        )
        peak = peak.astype(bf16).astype(f32)
        kept_w = jnp.where(use_kept, jnp.exp(kept_scores - peak), 0.0).astype(bf16)
        moved_w = jnp.where(use_moved, jnp.exp(moved_scores - peak), 0.0).astype(bf16)
        numerator = nt_dot(kept_w, kept[:LATENT]) + nt_dot(moved_w, moved[:LATENT])
        total = jnp.sum(kept_w.astype(f32) + moved_w.astype(f32), axis=1, keepdims=True)
        high = total.astype(bf16).astype(f32)
        stats = jnp.where(
            lane == 0, peak, jnp.where(lane == 1, high, jnp.where(lane == 2, total - high, 0.0))
        )
        both = jnp.concatenate([numerator, stats], axis=1)
        parts += [both[:HEADS], both[HEADS:]]
    by_head = jnp.transpose(jnp.stack(parts), (1, 0, 2))
    tiles = [by_head[:, :, i * LANES : (i + 1) * LANES] for i in range(5)]
    tiles.append(jnp.zeros_like(tiles[0]))
    for i in range(3):
        pair = jnp.concatenate([tiles[2 * i], tiles[2 * i + 1]], axis=1)
        out[:, 16 * i : 16 * (i + 1), :] = pair.astype(bf16)
    copy.wait()


def roll_kernel(pairing, chunks, partials, out):
    offset = pairing[lax.axis_index("tensor"), 0]
    out[:, 0:NROWS, :] = partials[...]
    for r in range(MEMBERS):
        source = lax.rem(r + MEMBERS - offset, MEMBERS)
        out[r, NROWS : NROWS + CHUNK, :] = chunks[source, VROWS : VROWS + CHUNK, :]


def merge_kernel(partials, w_value, out):
    rows = partials[...].astype(f32)
    stats = rows[:, 32:40, :]
    peak = stats[:, :, 0:1]
    top = jnp.max(peak, axis=0, keepdims=True)
    factor = jnp.exp(peak - top)
    total = jnp.sum(factor * (stats[:, :, 1:2] + stats[:, :, 2:3]), axis=0)
    weights = w_value[...].reshape(LATENT, LANES)
    values = jnp.zeros((REQ * STEPS, LANES), f32)
    for i in range(4):
        numerator = jnp.sum(factor * rows[:, 8 * i : 8 * (i + 1), :], axis=0)
        latent = (numerator / total).astype(bf16)
        values += jnp.dot(
            latent, weights[i * LANES : (i + 1) * LANES], preferred_element_type=f32
        )
    out[...] = jnp.broadcast_to(values.astype(bf16)[None], out.shape)


def project_kernel(values, w_out, out):
    flat = jnp.concatenate([values[h] for h in range(HEADS)], axis=1)
    for i in range(TENSOR):
        out[i] = nt_dot(flat, w_out[OUTC * i : OUTC * (i + 1), :])


def fill_kernel(cache_in, received, cache, sems):
    copies = []
    for b in range(REQ):
        for k in range(2):
            lane = SLICE + k * LANES
            copies.append(
                pltpu.make_async_copy(
                    received.at[b, k], cache.at[b, :, lane : lane + LANES], sems.at[b, k]
                )
            )
    for copy in copies:
        copy.start()
    for copy in copies:
        copy.wait()


def body(staying_cache, leaving_cache, lengths, pairing, new_entries, queries, w_value, w_out):
    staying = jnp.swapaxes(staying_cache[0], 1, 2)
    leaving = jnp.swapaxes(leaving_cache[0], 1, 2)
    q = queries.reshape(REQ, STEPS * HEADS, WIDTH)

    first = pl.pallas_call(
        pack_kernel,
        out_shape=jax.ShapeDtypeStruct((MEMBERS, VROWS + CHUNK, LANES), bf16),
        in_specs=[SMEM, VMEM, ANY, VMEM],
        out_specs=VMEM,
        scratch_shapes=[pltpu.VMEM((WIDTH, SLICE), bf16), pltpu.SemaphoreType.DMA],
        name="pack",
    )(lengths, new_entries, leaving, w_value)
    chunks = lax.all_to_all(first, "context", 0, 0)

    partials, cache = pl.pallas_call(
        attention_kernel,
        out_shape=(
            jax.ShapeDtypeStruct((MEMBERS, NROWS, LANES), bf16),
            jax.ShapeDtypeStruct((REQ, WIDTH, 2 * SLICE), bf16),
        ),
        in_specs=[SMEM, VMEM, VMEM, VMEM, VMEM],
        out_specs=(VMEM, ANY),
        scratch_shapes=[pltpu.SemaphoreType.DMA],
        cost_estimate=pl.CostEstimate(
            flops=300_000_000, bytes_accessed=8_000_000, transcendentals=65536
        ),
        name="attend",
    )(lengths, new_entries, q, staying, leaving)

    second = pl.pallas_call(
        roll_kernel,
        out_shape=jax.ShapeDtypeStruct((MEMBERS, NROWS + CHUNK, LANES), bf16),
        in_specs=[SMEM, VMEM, VMEM],
        out_specs=VMEM,
        name="roll",
    )(pairing, chunks, partials)
    arrived = lax.all_to_all(second, "context", 0, 0)

    received = lax.all_gather(arrived[:, NROWS:, :], "tensor")
    received = received.reshape(REQ, 2, WIDTH, LANES)

    values = pl.pallas_call(
        merge_kernel,
        out_shape=jax.ShapeDtypeStruct((MEMBERS, REQ * STEPS, LANES), bf16),
        grid=(1,),
        in_specs=[
            pl.BlockSpec((MEMBERS, NROWS, LANES), lambda i: (0, 0, 0)),
            pl.BlockSpec((MEMBERS, VROWS, LANES), lambda i: (0, 0, 0)),
        ],
        out_specs=pl.BlockSpec((MEMBERS, REQ * STEPS, LANES), lambda i: (0, 0, 0)),
        name="merge",
    )(arrived, chunks)
    all_values = lax.all_to_all(values, "context", 0, 0)

    columns = pl.pallas_call(
        project_kernel,
        out_shape=jax.ShapeDtypeStruct((TENSOR, REQ * STEPS, OUTC), f32),
        in_specs=[VMEM, VMEM],
        out_specs=VMEM,
        name="project",
    )(all_values, w_out.T)
    terms = lax.all_to_all(columns, "tensor", 0, 0)
    attn_out = jnp.sum(terms, axis=0).astype(bf16).reshape(REQ, STEPS, OUTC)

    cache = pl.pallas_call(
        fill_kernel,
        out_shape=jax.ShapeDtypeStruct((REQ, WIDTH, 2 * SLICE), bf16),
        in_specs=[ANY, ANY],
        out_specs=ANY,
        scratch_shapes=[pltpu.SemaphoreType.DMA((REQ, 2))],
        input_output_aliases={0: 0},
        name="fill",
    )(cache, received)
    return (jnp.swapaxes(cache, 1, 2)[None], attn_out)


def solution(mesh):
    placed = (
        P("context", "dp", None, None),
        P("context", "dp", None, None),
        P("dp"),
        P("dp", None),
        P("dp", None, None),
        P("dp", None, "tensor", None),
        P("tensor", "context", None),
        P("tensor", "context"),
    )
    return jax.shard_map(
        body,
        mesh=mesh,
        in_specs=placed,
        out_specs=(P("context", "dp", None, None), P("dp", None, ("context", "tensor"))),
        check_vma=False,
    )
```

```python
import jax
import jax.numpy as jnp
from jax import lax
from jax.experimental import pallas as pl
from jax.experimental.pallas import tpu as pltpu
from jax.sharding import PartitionSpec as P

REQ = 4
STEPS = 2
HEADS = 16
LATENT = 512
WIDTH = 576
SLICE = 256
MEMBERS = 16
TENSOR = 4
LANES = 128
CHUNK = WIDTH * SLICE // (MEMBERS * LANES)
VROWS = LATENT // MEMBERS
NROWS = 48
OUTC = 112

softmax_scale = 0.07216878364870322
large_negative = -1e30

f32 = jnp.float32
bf16 = jnp.bfloat16

VMEM = pl.BlockSpec(memory_space=pltpu.VMEM)
SMEM = pl.BlockSpec(memory_space=pltpu.SMEM)
ANY = pl.BlockSpec(memory_space=pl.ANY)


def nt_dot(a, b):
    return lax.dot_general(a, b, (((1,), (1,)), ((), ())), preferred_element_type=f32)


def with_new_entries(block, entries, length, member):
    first = (MEMBERS + member) * SLICE
    slot = lax.broadcasted_iota(jnp.int32, (STEPS, SLICE), 1)
    step = lax.broadcasted_iota(jnp.int32, (STEPS, SLICE), 0)
    hit = (slot + first == length + step).astype(f32)
    placed = lax.dot_general(
        entries, hit.astype(bf16), (((0,), (0,)), ((), ())), preferred_element_type=f32
    )
    taken = jnp.max(hit, axis=0, keepdims=True) > 0.5
    return jnp.where(taken, placed, block.astype(f32)).astype(bf16)


def update_kernel(lengths, entries, leaving, out):
    tensor = lax.axis_index("tensor")
    member = lax.axis_index("context")
    out[...] = with_new_entries(leaving[0], entries[tensor], lengths[tensor], member)


def attention_kernel(lengths, entries, queries, staying, leaving, w_value, out):
    member = lax.axis_index("context")
    out[:, NROWS : NROWS + VROWS, :] = w_value[...]
    row = lax.broadcasted_iota(jnp.int32, (STEPS * HEADS, SLICE), 0)
    slot = lax.broadcasted_iota(jnp.int32, (STEPS * HEADS, SLICE), 1)
    step = (row >= HEADS).astype(jnp.int32)
    lane = lax.broadcasted_iota(jnp.int32, (STEPS * HEADS, LANES), 1)
    parts = []
    for b in range(REQ):
        q = queries[b]
        kept = staying[b]
        moved = with_new_entries(leaving[b], entries[b], lengths[b], member)
        limit = lengths[b] + 1 + step
        use_kept = slot + member * SLICE < limit
        use_moved = slot + (MEMBERS + member) * SLICE < limit
        kept_scores = jnp.dot(q, kept, preferred_element_type=f32) * softmax_scale
        moved_scores = jnp.dot(q, moved, preferred_element_type=f32) * softmax_scale
        kept_scores = jnp.where(use_kept, kept_scores, large_negative)
        moved_scores = jnp.where(use_moved, moved_scores, large_negative)
        peak = jnp.maximum(
            jnp.max(kept_scores, axis=1, keepdims=True),
            jnp.max(moved_scores, axis=1, keepdims=True),
        )
        peak = peak.astype(bf16).astype(f32)
        kept_w = jnp.where(use_kept, jnp.exp(kept_scores - peak), 0.0).astype(bf16)
        moved_w = jnp.where(use_moved, jnp.exp(moved_scores - peak), 0.0).astype(bf16)
        numerator = nt_dot(kept_w, kept[:LATENT]) + nt_dot(moved_w, moved[:LATENT])
        total = jnp.sum(kept_w.astype(f32) + moved_w.astype(f32), axis=1, keepdims=True)
        high = total.astype(bf16).astype(f32)
        stats = jnp.where(
            lane == 0, peak, jnp.where(lane == 1, high, jnp.where(lane == 2, total - high, 0.0))
        )
        both = jnp.concatenate([numerator, stats], axis=1)
        parts += [both[:HEADS], both[HEADS:]]
    by_head = jnp.transpose(jnp.stack(parts), (1, 0, 2))
    tiles = [by_head[:, :, i * LANES : (i + 1) * LANES] for i in range(5)]
    tiles.append(jnp.zeros_like(tiles[0]))
    for i in range(3):
        pair = jnp.concatenate([tiles[2 * i], tiles[2 * i + 1]], axis=1)
        out[:, 16 * i : 16 * (i + 1), :] = pair.astype(bf16)


def merge_kernel(arrived, out):
    rows = arrived[:, 0:NROWS, :].astype(f32)
    stats = rows[:, 32:40, :]
    peak = stats[:, :, 0:1]
    top = jnp.max(peak, axis=0, keepdims=True)
    factor = jnp.exp(peak - top)
    total = jnp.sum(factor * (stats[:, :, 1:2] + stats[:, :, 2:3]), axis=0)
    weights = arrived[:, NROWS : NROWS + VROWS, :].reshape(LATENT, LANES)
    values = jnp.zeros((REQ * STEPS, LANES), f32)
    for i in range(4):
        numerator = jnp.sum(factor * rows[:, 8 * i : 8 * (i + 1), :], axis=0)
        latent = (numerator / total).astype(bf16)
        values += jnp.dot(
            latent, weights[i * LANES : (i + 1) * LANES], preferred_element_type=f32
        )
    out[...] = jnp.broadcast_to(values.astype(bf16)[None], out.shape)


def project_kernel(values, w_out, out):
    flat = jnp.concatenate([values[h] for h in range(HEADS)], axis=1)
    for i in range(TENSOR):
        out[i] = nt_dot(flat, w_out[OUTC * i : OUTC * (i + 1), :])


def keep_kernel(staying, columns, cache, sem):
    copy = pltpu.make_async_copy(staying, cache.at[:, :, 0:SLICE], sem)
    copy.start()
    copy.wait()


def fill_kernel(cache_in, received, cache, sem):
    copy = pltpu.make_async_copy(received, cache.at[:, :, SLICE : 2 * SLICE], sem)
    copy.start()
    copy.wait()


def attend(lengths, entries, queries, staying, leaving, w_value):
    return pl.pallas_call(
        attention_kernel,
        out_shape=jax.ShapeDtypeStruct((MEMBERS, NROWS + VROWS, LANES), bf16),
        in_specs=[SMEM, VMEM, VMEM, VMEM, VMEM, VMEM],
        out_specs=VMEM,
        cost_estimate=pl.CostEstimate(
            flops=300_000_000, bytes_accessed=4_000_000, transcendentals=65536
        ),
        name="attend",
    )(lengths, entries, queries, staying, leaving, w_value)


def exchange(distance):
    route = [((r - distance) % MEMBERS, r) for r in range(MEMBERS)]

    def branch(block, *operands):
        moved = lax.ppermute(block, "context", route) if distance else block
        return moved, lax.all_to_all(attend(*operands), "context", 0, 0)

    return branch


def body(staying_cache, leaving_cache, lengths, pairing, new_entries, queries, w_value, w_out):
    staying = jnp.swapaxes(staying_cache[0], 1, 2)
    leaving = jnp.swapaxes(leaving_cache[0], 1, 2)
    q = queries.reshape(REQ, STEPS * HEADS, WIDTH)
    tensor = lax.axis_index("tensor")

    block = pl.pallas_call(
        update_kernel,
        out_shape=jax.ShapeDtypeStruct((WIDTH, SLICE), bf16),
        grid=(1,),
        in_specs=[
            SMEM,
            VMEM,
            pl.BlockSpec((1, WIDTH, SLICE), lambda i: (lax.axis_index("tensor"), 0, 0)),
        ],
        out_specs=VMEM,
        name="update",
    )(lengths, new_entries, leaving)

    offset = lax.dynamic_index_in_dim(pairing[:, 0], tensor, 0, False) % MEMBERS
    moved, arrived = lax.switch(
        offset,
        [exchange(d) for d in range(MEMBERS)],
        block, lengths, new_entries, q, staying, leaving, w_value,
    )
    received = lax.all_gather(moved, "tensor")

    values = pl.pallas_call(
        merge_kernel,
        out_shape=jax.ShapeDtypeStruct((MEMBERS, REQ * STEPS, LANES), bf16),
        in_specs=[VMEM],
        out_specs=VMEM,
        name="merge",
    )(arrived)
    all_values = lax.all_to_all(values, "context", 0, 0)

    columns = pl.pallas_call(
        project_kernel,
        out_shape=jax.ShapeDtypeStruct((TENSOR, REQ * STEPS, OUTC), f32),
        in_specs=[VMEM, VMEM],
        out_specs=VMEM,
        name="project",
    )(all_values, w_out.T)
    terms = lax.all_to_all(columns, "tensor", 0, 0)
    attn_out = jnp.sum(terms, axis=0).astype(bf16).reshape(REQ, STEPS, OUTC)

    cache = pl.pallas_call(
        keep_kernel,
        out_shape=jax.ShapeDtypeStruct((REQ, WIDTH, 2 * SLICE), bf16),
        in_specs=[VMEM, ANY],
        out_specs=ANY,
        scratch_shapes=[pltpu.SemaphoreType.DMA],
        cost_estimate=pl.CostEstimate(flops=0, bytes_accessed=8_000_000, transcendentals=0),
        name="keep",
    )(staying, columns)
    cache = pl.pallas_call(
        fill_kernel,
        out_shape=jax.ShapeDtypeStruct((REQ, WIDTH, 2 * SLICE), bf16),
        in_specs=[ANY, VMEM],
        out_specs=ANY,
        scratch_shapes=[pltpu.SemaphoreType.DMA],
        input_output_aliases={0: 0},
        name="fill",
    )(cache, received)
    return (jnp.swapaxes(cache, 1, 2)[None], attn_out)


def solution(mesh):
    placed = (
        P("context", "dp", None, None),
        P("context", "dp", None, None),
        P("dp"),
        P("dp", None),
        P("dp", None, None),
        P("dp", None, "tensor", None),
        P("tensor", "context", None),
        P("tensor", "context"),
    )
    return jax.shard_map(
        body,
        mesh=mesh,
        in_specs=placed,
        out_specs=(P("context", "dp", None, None), P("dp", None, ("context", "tensor"))),
        check_vma=False,
    )
```

```python
import jax
import jax.numpy as jnp
from jax import lax
from jax.experimental import pallas as pl
from jax.experimental.pallas import tpu as pltpu
from jax.sharding import PartitionSpec as P

REQ = 4
STEPS = 2
HEADS = 16
LATENT = 512
WIDTH = 576
SLICE = 256
MEMBERS = 16
TENSOR = 4
LANES = 128
CHUNK = WIDTH * SLICE // (MEMBERS * LANES)
ROWS = REQ * STEPS
LTILES = LATENT // LANES
VROWS = LATENT // MEMBERS
STATS = LTILES * ROWS
VALUE = STATS + ROWS
CACHE = VALUE + VROWS
OUTC = 112
PART = 2 * ROWS
PIECES = 2
PIECE = WIDTH // PIECES
FORTH_0 = 0
FORTH_FAR = WIDTH
FORTH_NEAR = FORTH_FAR + PART
FORTH_1 = FORTH_NEAR + PART
FORTH_ROWS = FORTH_1 + WIDTH
BACK_0 = PART
BACK_1 = BACK_0 + WIDTH
BACK_ROWS = BACK_1 + WIDTH

softmax_scale = 0.07216878364870322
large_negative = -1e30

f32 = jnp.float32
bf16 = jnp.bfloat16

VMEM = pl.BlockSpec(memory_space=pltpu.VMEM)
SMEM = pl.BlockSpec(memory_space=pltpu.SMEM)
ANY = pl.BlockSpec(memory_space=pl.ANY)


def nt_dot(a, b):
    return lax.dot_general(a, b, (((1,), (1,)), ((), ())), preferred_element_type=f32)


def attend_kernel(
    lengths, entries, queries, staying_hbm, leaving_hbm, w_value, out, staying, leaving, sems
):
    member = lax.axis_index("context")
    tensor = lax.axis_index("tensor")
    copies = []
    for b in range(REQ):
        copies.append(
            (
                pltpu.make_async_copy(staying_hbm.at[b], staying.at[b], sems.at[0, b]),
                pltpu.make_async_copy(leaving_hbm.at[b], leaving.at[b], sems.at[1, b]),
            )
        )
    for pair in copies:
        for copy in pair:
            copy.start()
    out[:, VALUE : VALUE + VROWS, :] = w_value[...]
    first_kept = member * SLICE
    first_moved = (MEMBERS + member) * SLICE
    row = lax.broadcasted_iota(jnp.int32, (STEPS * HEADS, SLICE), 0)
    slot = lax.broadcasted_iota(jnp.int32, (STEPS * HEADS, SLICE), 1)
    step = (row >= HEADS).astype(jnp.int32)
    lane = lax.broadcasted_iota(jnp.int32, (STEPS * HEADS, LANES), 1)
    parts = []
    for b in range(REQ):
        for copy in copies[b]:
            copy.wait()
        new_slot = lengths[b] - first_moved

        @pl.when((new_slot + STEPS > 0) & (new_slot < SLICE))
        def _():
            slots = lax.broadcasted_iota(jnp.int32, (STEPS, SLICE), 1)
            steps = lax.broadcasted_iota(jnp.int32, (STEPS, SLICE), 0)
            hit = (slots == new_slot + steps).astype(f32)
            placed = lax.dot_general(
                entries[b], hit.astype(bf16), (((0,), (0,)), ((), ())), preferred_element_type=f32
            )
            taken = jnp.max(hit, axis=0, keepdims=True) > 0.5
            leaving[b] = jnp.where(taken, placed, leaving[b].astype(f32)).astype(bf16)

        q = queries[b]
        limit = lengths[b] + 1 + step
        use_kept = slot + first_kept < limit
        use_moved = slot + first_moved < limit
        kept_scores = jnp.dot(q, staying[b], preferred_element_type=f32) * softmax_scale
        moved_scores = jnp.dot(q, leaving[b], preferred_element_type=f32) * softmax_scale
        kept_scores = jnp.where(use_kept, kept_scores, large_negative)
        moved_scores = jnp.where(use_moved, moved_scores, large_negative)
        peak = jnp.maximum(
            jnp.max(kept_scores, axis=1, keepdims=True),
            jnp.max(moved_scores, axis=1, keepdims=True),
        )
        peak = peak.astype(bf16).astype(f32)
        kept_w = jnp.where(use_kept, jnp.exp(kept_scores - peak), 0.0).astype(bf16)
        moved_w = jnp.where(use_moved, jnp.exp(moved_scores - peak), 0.0).astype(bf16)
        numerator = nt_dot(kept_w, staying[b, 0:LATENT, :]) + nt_dot(
            moved_w, leaving[b, 0:LATENT, :]
        )
        total = jnp.sum(kept_w.astype(f32) + moved_w.astype(f32), axis=1, keepdims=True)
        high = total.astype(bf16).astype(f32)
        stats = jnp.where(
            lane == 0, peak, jnp.where(lane == 1, high, jnp.where(lane == 2, total - high, 0.0))
        )
        both = jnp.concatenate([numerator, stats], axis=1)
        parts += [both[:HEADS], both[HEADS:]]
    by_head = jnp.transpose(jnp.stack(parts), (1, 0, 2))
    tiles = [by_head[:, :, i * LANES : (i + 1) * LANES] for i in range(LTILES + 1)]
    out[:, 0:VALUE, :] = jnp.concatenate(tiles, axis=1).astype(bf16)
    block = leaving[tensor]
    for c in range(MEMBERS):
        at, lanes = (c % 8) * CHUNK, (c // 8) * LANES
        out[c, CACHE : CACHE + CHUNK, :] = block[at : at + CHUNK, lanes : lanes + LANES]


def merge_kernel(pairing, arrived, out):
    offset = pairing[lax.axis_index("tensor"), 0]
    rows = arrived[:, 0:VALUE, :].astype(f32)
    stats = rows[:, STATS:VALUE, :]
    peak = stats[:, :, 0:1]
    top = jnp.max(peak, axis=0, keepdims=True)
    factor = jnp.exp(peak - top)
    total = jnp.sum(factor * (stats[:, :, 1:2] + stats[:, :, 2:3]), axis=0)
    weights = arrived[:, VALUE : VALUE + VROWS, :].reshape(LATENT, LANES)
    values = jnp.zeros((ROWS, LANES), f32)
    for i in range(LTILES):
        numerator = jnp.sum(factor * rows[:, ROWS * i : ROWS * (i + 1), :], axis=0)
        latent = (numerator / total).astype(bf16)
        values += jnp.dot(
            latent, weights[i * LANES : (i + 1) * LANES], preferred_element_type=f32
        )
    values = values.astype(bf16)
    for r in range(MEMBERS):
        source = lax.rem(r + MEMBERS - offset, MEMBERS)
        out[r, 0:CHUNK, :] = arrived[source, CACHE : CACHE + CHUNK, :]
        out[r, CHUNK : CHUNK + ROWS, :] = values


def project_kernel(handed, w_out, forth, back, mine):
    tensor = lax.axis_index("tensor")
    for c in range(MEMBERS):
        at = CHUNK * (c % 8)
        forth[(FORTH_0, FORTH_1)[c // 8] + at : (FORTH_0, FORTH_1)[c // 8] + at + CHUNK, :] = (
            handed[c, 0:CHUNK, :]
        )
        back[(BACK_0, BACK_1)[c // 8] + at : (BACK_0, BACK_1)[c // 8] + at + CHUNK, :] = (
            handed[c, 0:CHUNK, :]
        )
    flat = jnp.concatenate([handed[h, CHUNK : CHUNK + ROWS, :] for h in range(HEADS)], axis=1)
    columns = nt_dot(flat, w_out[...])
    pad = jnp.zeros((ROWS, LANES - OUTC), f32)
    parts = [
        jnp.concatenate([columns[:, OUTC * t : OUTC * (t + 1)], pad], axis=1)
        for t in range(TENSOR)
    ]

    def part_of(distance):
        target = lax.rem(tensor + distance, TENSOR)
        part = parts[0]
        for t in range(1, TENSOR):
            part = jnp.where(target == t, parts[t], part)
        return part

    def pieces(part):
        high = part.astype(bf16)
        return jnp.concatenate([high, (part - high.astype(f32)).astype(bf16)], axis=0)

    mine[...] = part_of(0)
    forth[FORTH_NEAR : FORTH_NEAR + PART, :] = pieces(part_of(1))
    forth[FORTH_FAR : FORTH_FAR + PART, :] = pieces(part_of(2))
    back[0:PART, :] = pieces(part_of(3))


def stores(block, first, cache, request, half, sems):
    lanes = SLICE + half * LANES
    return [
        pltpu.make_async_copy(
            block.at[first + PIECE * i : first + PIECE * (i + 1), :],
            cache.at[request, PIECE * i : PIECE * (i + 1), lanes : lanes + LANES],
            sems.at[i],
        )
        for i in range(PIECES)
    ]


def finish_all(copies):
    for copy in copies:
        copy.start()
    for copy in copies:
        copy.wait()


def keep_kernel(staying, forth, cache, sem, sems):
    tensor = lax.axis_index("tensor")
    finish_all(
        [pltpu.make_async_copy(staying, cache.at[:, :, 0:SLICE], sem)]
        + stores(forth, FORTH_0, cache, tensor, 0, sems.at[0])
        + stores(forth, FORTH_1, cache, tensor, 1, sems.at[1])
    )


def joined(pieces):
    pieces = pieces.astype(f32)
    return pieces[:ROWS] + pieces[ROWS:]


def near_kernel(cache_in, from_left, from_right, mine, cache, total, sems):
    tensor = lax.axis_index("tensor")
    left = lax.rem(tensor + TENSOR - 1, TENSOR)
    right = lax.rem(tensor + 1, TENSOR)
    total[...] = (
        mine[...]
        + joined(from_left[FORTH_NEAR : FORTH_NEAR + PART, :])
        + joined(from_right[0:PART, :])
    )
    finish_all(
        stores(from_left, FORTH_0, cache, left, 0, sems.at[0])
        + stores(from_left, FORTH_1, cache, left, 1, sems.at[1])
        + stores(from_right, BACK_0, cache, right, 0, sems.at[2])
        + stores(from_right, BACK_1, cache, right, 1, sems.at[3])
    )


def far_kernel(cache_in, far_left, far_right, near_total, cache, attn, sems):
    across = lax.rem(lax.axis_index("tensor") + 2, TENSOR)
    copies = stores(far_left, 0, cache, across, 0, sems.at[0])
    copies += stores(far_right, 0, cache, across, 1, sems.at[1])
    for copy in copies:
        copy.start()
    total = near_total[...] + joined(far_left[FORTH_FAR : FORTH_FAR + PART, :])
    attn[...] = total[:, :OUTC].astype(bf16)
    for copy in copies:
        copy.wait()


def body(staying_cache, leaving_cache, lengths, pairing, new_entries, queries, w_value, w_out):
    staying = jnp.swapaxes(staying_cache[0], 1, 2)
    leaving = jnp.swapaxes(leaving_cache[0], 1, 2)
    q = queries.reshape(REQ, STEPS * HEADS, WIDTH)

    first = pl.pallas_call(
        attend_kernel,
        out_shape=jax.ShapeDtypeStruct((MEMBERS, CACHE + CHUNK, LANES), bf16),
        in_specs=[SMEM, VMEM, VMEM, ANY, ANY, VMEM],
        out_specs=VMEM,
        scratch_shapes=[
            pltpu.VMEM((REQ, WIDTH, SLICE), bf16),
            pltpu.VMEM((REQ, WIDTH, SLICE), bf16),
            pltpu.SemaphoreType.DMA((2, REQ)),
        ],
        name="attend",
    )(lengths, new_entries, q, staying, leaving, w_value)
    arrived = lax.all_to_all(first, "context", 0, 0)

    second = pl.pallas_call(
        merge_kernel,
        out_shape=jax.ShapeDtypeStruct((MEMBERS, CHUNK + ROWS, LANES), bf16),
        in_specs=[SMEM, VMEM],
        out_specs=VMEM,
        name="merge",
    )(pairing, arrived)
    handed = lax.all_to_all(second, "context", 0, 0)

    forth, back, mine = pl.pallas_call(
        project_kernel,
        out_shape=(
            jax.ShapeDtypeStruct((FORTH_ROWS, LANES), bf16),
            jax.ShapeDtypeStruct((BACK_ROWS, LANES), bf16),
            jax.ShapeDtypeStruct((ROWS, LANES), f32),
        ),
        in_specs=[VMEM, VMEM],
        out_specs=(VMEM, VMEM, VMEM),
        name="project",
    )(handed, w_out.T)

    up = [((t - 1) % TENSOR, t) for t in range(TENSOR)]
    down = [((t + 1) % TENSOR, t) for t in range(TENSOR)]
    from_left = lax.ppermute(forth, "tensor", up)
    from_right = lax.ppermute(back, "tensor", down)
    far_left = lax.ppermute(from_left[0 : FORTH_FAR + PART], "tensor", up)
    far_right = lax.ppermute(from_right[BACK_1:], "tensor", down)

    whole = jax.ShapeDtypeStruct((REQ, WIDTH, 2 * SLICE), bf16)
    cache = pl.pallas_call(
        keep_kernel,
        out_shape=whole,
        in_specs=[VMEM, VMEM],
        out_specs=ANY,
        scratch_shapes=[pltpu.SemaphoreType.DMA, pltpu.SemaphoreType.DMA((2, PIECES))],
        cost_estimate=pl.CostEstimate(flops=0, bytes_accessed=8_000_000, transcendentals=0),
        name="keep",
    )(staying, forth)
    cache, near_total = pl.pallas_call(
        near_kernel,
        out_shape=(whole, jax.ShapeDtypeStruct((ROWS, LANES), f32)),
        in_specs=[ANY, VMEM, VMEM, VMEM],
        out_specs=(ANY, VMEM),
        scratch_shapes=[pltpu.SemaphoreType.DMA((4, PIECES))],
        input_output_aliases={0: 0},
        cost_estimate=pl.CostEstimate(flops=0, bytes_accessed=4_000_000, transcendentals=0),
        name="near",
    )(cache, from_left, from_right, mine)
    cache, attn_out = pl.pallas_call(
        far_kernel,
        out_shape=(whole, jax.ShapeDtypeStruct((ROWS, OUTC), bf16)),
        in_specs=[ANY, VMEM, VMEM, VMEM],
        out_specs=(ANY, VMEM),
        scratch_shapes=[pltpu.SemaphoreType.DMA((2, PIECES))],
        input_output_aliases={0: 0},
        name="far",
    )(cache, far_left, far_right, near_total)
    attn_out = attn_out.reshape(REQ, STEPS, OUTC)
    return (jnp.swapaxes(cache, 1, 2)[None], attn_out)


def solution(mesh):
    placed = (
        P("context", "dp", None, None),
        P("context", "dp", None, None),
        P("dp"),
        P("dp", None),
        P("dp", None, None),
        P("dp", None, "tensor", None),
        P("tensor", "context", None),
        P("tensor", "context"),
    )
    return jax.shard_map(
        body,
        mesh=mesh,
        in_specs=placed,
        out_specs=(P("context", "dp", None, None), P("dp", None, ("context", "tensor"))),
        check_vma=False,
    )
```

```python
import jax
import jax.numpy as jnp
from jax import lax
from jax.experimental import pallas as pl
from jax.experimental.pallas import tpu as pltpu
from jax.sharding import PartitionSpec as P

REQ = 4
STEPS = 2
HEADS = 16
LATENT = 512
WIDTH = 576
SLICE = 256
MEMBERS = 16
TENSOR = 4
LANES = 128
CHUNK = WIDTH * SLICE // (MEMBERS * LANES)
ROWS = REQ * STEPS
LTILES = LATENT // LANES
VROWS = LATENT // MEMBERS
STATS = LTILES * ROWS
CACHE = VROWS
PARTIAL = CACHE + CHUNK
SENT = PARTIAL + STATS + ROWS
EARLY = 96
OUTC = 112
PART = 2 * ROWS
PIECES = 2
PIECE = WIDTH // PIECES
FORTH_0 = 0
FORTH_FAR = WIDTH
FORTH_NEAR = FORTH_FAR + PART
FORTH_1 = FORTH_NEAR + PART
FORTH_ROWS = FORTH_1 + WIDTH
BACK_0 = PART
BACK_1 = BACK_0 + WIDTH
BACK_ROWS = BACK_1 + WIDTH

softmax_scale = 0.07216878364870322
large_negative = -1e30

f32 = jnp.float32
bf16 = jnp.bfloat16

VMEM = pl.BlockSpec(memory_space=pltpu.VMEM)
SMEM = pl.BlockSpec(memory_space=pltpu.SMEM)
ANY = pl.BlockSpec(memory_space=pl.ANY)


def grant(mib):
    return pltpu.CompilerParams(vmem_limit_bytes=mib * 2**20)


def nt_dot(a, b):
    return lax.dot_general(a, b, (((1,), (1,)), ((), ())), preferred_element_type=f32)


def attend_kernel(
    lengths,
    entries,
    queries_hbm,
    staying_hbm,
    leaving_hbm,
    w_value_hbm,
    out_hbm,
    queries,
    staying,
    leaving,
    w_value,
    out,
    sems,
):
    member = lax.axis_index("context")
    tensor = lax.axis_index("tensor")
    kept_copies, moved_copies = [], []
    for b in range(REQ):
        moved_copies.append(
            pltpu.make_async_copy(leaving_hbm.at[b], leaving.at[b], sems.at[0, b])
        )
        moved_copies[b].start()
    query_copy = pltpu.make_async_copy(queries_hbm, queries, sems.at[2, 0])
    query_copy.start()
    value_copy = pltpu.make_async_copy(w_value_hbm, w_value, sems.at[2, 1])
    value_copy.start()
    for b in range(REQ):
        kept_copies.append(
            pltpu.make_async_copy(staying_hbm.at[b], staying.at[b], sems.at[1, b])
        )
        kept_copies[b].start()
    first_kept = member * SLICE
    first_moved = (MEMBERS + member) * SLICE
    row = lax.broadcasted_iota(jnp.int32, (STEPS * HEADS, SLICE), 0)
    slot = lax.broadcasted_iota(jnp.int32, (STEPS * HEADS, SLICE), 1)
    step = (row >= HEADS).astype(jnp.int32)
    lane = lax.broadcasted_iota(jnp.int32, (STEPS * HEADS, LANES), 1)
    parts = []
    for b in range(REQ):
        moved_copies[b].wait()
        new_slot = lengths[b] - first_moved

        @pl.when((new_slot + STEPS > 0) & (new_slot < SLICE))
        def _():
            slots = lax.broadcasted_iota(jnp.int32, (STEPS, SLICE), 1)
            steps = lax.broadcasted_iota(jnp.int32, (STEPS, SLICE), 0)
            hit = (slots == new_slot + steps).astype(f32)
            placed = lax.dot_general(
                entries[b], hit.astype(bf16), (((0,), (0,)), ((), ())), preferred_element_type=f32
            )
            taken = jnp.max(hit, axis=0, keepdims=True) > 0.5
            leaving[b] = jnp.where(taken, placed, leaving[b].astype(f32)).astype(bf16)

    block = leaving[tensor]
    for c in range(MEMBERS):
        at, lanes = (c % 8) * CHUNK, (c // 8) * LANES
        out[c, CACHE : CACHE + CHUNK, :] = block[at : at + CHUNK, lanes : lanes + LANES]
    value_copy.wait()
    out[:, 0:VROWS, :] = w_value[...]
    early_copy = pltpu.make_async_copy(
        out.at[:, 0:EARLY, :], out_hbm.at[:, 0:EARLY, :], sems.at[2, 2]
    )
    early_copy.start()
    query_copy.wait()
    for b in range(REQ):
        kept_copies[b].wait()
        q = queries[b]
        limit = lengths[b] + 1 + step
        use_kept = slot + first_kept < limit
        use_moved = slot + first_moved < limit
        kept_scores = jnp.dot(q, staying[b], preferred_element_type=f32) * softmax_scale
        moved_scores = jnp.dot(q, leaving[b], preferred_element_type=f32) * softmax_scale
        kept_scores = jnp.where(use_kept, kept_scores, large_negative)
        moved_scores = jnp.where(use_moved, moved_scores, large_negative)
        peak = jnp.maximum(
            jnp.max(kept_scores, axis=1, keepdims=True),
            jnp.max(moved_scores, axis=1, keepdims=True),
        )
        peak = peak.astype(bf16).astype(f32)
        kept_w = jnp.where(use_kept, jnp.exp(kept_scores - peak), 0.0).astype(bf16)
        moved_w = jnp.where(use_moved, jnp.exp(moved_scores - peak), 0.0).astype(bf16)
        numerator = nt_dot(kept_w, staying[b, 0:LATENT, :]) + nt_dot(
            moved_w, leaving[b, 0:LATENT, :]
        )
        total = jnp.sum(kept_w.astype(f32) + moved_w.astype(f32), axis=1, keepdims=True)
        high = total.astype(bf16).astype(f32)
        stats = jnp.where(
            lane == 0, peak, jnp.where(lane == 1, high, jnp.where(lane == 2, total - high, 0.0))
        )
        both = jnp.concatenate([numerator, stats], axis=1)
        parts += [both[:HEADS], both[HEADS:]]
    by_head = jnp.transpose(jnp.stack(parts), (1, 0, 2))
    tiles = [by_head[:, :, i * LANES : (i + 1) * LANES] for i in range(LTILES + 1)]
    out[:, PARTIAL:SENT, :] = jnp.concatenate(tiles, axis=1).astype(bf16)
    late_copy = pltpu.make_async_copy(
        out.at[:, EARLY:SENT, :], out_hbm.at[:, EARLY:SENT, :], sems.at[2, 3]
    )
    late_copy.start()
    early_copy.wait()
    late_copy.wait()


def merge_kernel(pairing, arrived, out):
    offset = pairing[lax.axis_index("tensor"), 0]
    rows = arrived[:, PARTIAL:SENT, :].astype(f32)
    stats = rows[:, STATS:, :]
    peak = stats[:, :, 0:1]
    top = jnp.max(peak, axis=0, keepdims=True)
    factor = jnp.exp(peak - top)
    total = jnp.sum(factor * (stats[:, :, 1:2] + stats[:, :, 2:3]), axis=0)
    weights = arrived[:, 0:VROWS, :].reshape(LATENT, LANES)
    values = jnp.zeros((ROWS, LANES), f32)
    for i in range(LTILES):
        numerator = jnp.sum(factor * rows[:, ROWS * i : ROWS * (i + 1), :], axis=0)
        latent = (numerator / total).astype(bf16)
        values += jnp.dot(
            latent, weights[i * LANES : (i + 1) * LANES], preferred_element_type=f32
        )
    values = values.astype(bf16)
    for r in range(MEMBERS):
        source = lax.rem(r + MEMBERS - offset, MEMBERS)
        out[r, 0:CHUNK, :] = arrived[source, CACHE : CACHE + CHUNK, :]
        out[r, CHUNK : CHUNK + ROWS, :] = values


def project_kernel(handed, w_out, forth, back, mine):
    tensor = lax.axis_index("tensor")
    for c in range(MEMBERS):
        at = CHUNK * (c % 8)
        forth[(FORTH_0, FORTH_1)[c // 8] + at : (FORTH_0, FORTH_1)[c // 8] + at + CHUNK, :] = (
            handed[c, 0:CHUNK, :]
        )
        back[(BACK_0, BACK_1)[c // 8] + at : (BACK_0, BACK_1)[c // 8] + at + CHUNK, :] = (
            handed[c, 0:CHUNK, :]
        )
    flat = jnp.concatenate([handed[h, CHUNK : CHUNK + ROWS, :] for h in range(HEADS)], axis=1)
    columns = nt_dot(flat, w_out[...])
    pad = jnp.zeros((ROWS, LANES - OUTC), f32)
    parts = [
        jnp.concatenate([columns[:, OUTC * t : OUTC * (t + 1)], pad], axis=1)
        for t in range(TENSOR)
    ]

    def part_of(distance):
        target = lax.rem(tensor + distance, TENSOR)
        part = parts[0]
        for t in range(1, TENSOR):
            part = jnp.where(target == t, parts[t], part)
        return part

    def pieces(part):
        high = part.astype(bf16)
        return jnp.concatenate([high, (part - high.astype(f32)).astype(bf16)], axis=0)

    mine[...] = part_of(0)
    forth[FORTH_NEAR : FORTH_NEAR + PART, :] = pieces(part_of(1))
    forth[FORTH_FAR : FORTH_FAR + PART, :] = pieces(part_of(2))
    back[0:PART, :] = pieces(part_of(3))


def stores(block, first, cache, request, half, sems):
    lanes = SLICE + half * LANES
    return [
        pltpu.make_async_copy(
            block.at[first + PIECE * i : first + PIECE * (i + 1), :],
            cache.at[request, PIECE * i : PIECE * (i + 1), lanes : lanes + LANES],
            sems.at[i],
        )
        for i in range(PIECES)
    ]


def finish_all(copies):
    for copy in copies:
        copy.start()
    for copy in copies:
        copy.wait()


def keep_kernel(staying, forth, cache, sem, sems):
    tensor = lax.axis_index("tensor")
    finish_all(
        [pltpu.make_async_copy(staying, cache.at[:, :, 0:SLICE], sem)]
        + stores(forth, FORTH_0, cache, tensor, 0, sems.at[0])
        + stores(forth, FORTH_1, cache, tensor, 1, sems.at[1])
    )


def joined(pieces):
    pieces = pieces.astype(f32)
    return pieces[:ROWS] + pieces[ROWS:]


def near_kernel(cache_in, from_left, from_right, mine, cache, total, sems):
    tensor = lax.axis_index("tensor")
    left = lax.rem(tensor + TENSOR - 1, TENSOR)
    right = lax.rem(tensor + 1, TENSOR)
    total[...] = (
        mine[...]
        + joined(from_left[FORTH_NEAR : FORTH_NEAR + PART, :])
        + joined(from_right[0:PART, :])
    )
    finish_all(
        stores(from_left, FORTH_0, cache, left, 0, sems.at[0])
        + stores(from_left, FORTH_1, cache, left, 1, sems.at[1])
        + stores(from_right, BACK_0, cache, right, 0, sems.at[2])
        + stores(from_right, BACK_1, cache, right, 1, sems.at[3])
    )


def far_kernel(cache_in, far_left, far_right, near_total, cache, attn, sems):
    across = lax.rem(lax.axis_index("tensor") + 2, TENSOR)
    copies = stores(far_left, 0, cache, across, 0, sems.at[0])
    copies += stores(far_right, 0, cache, across, 1, sems.at[1])
    for copy in copies:
        copy.start()
    total = near_total[...] + joined(far_left[FORTH_FAR : FORTH_FAR + PART, :])
    attn[...] = total[:, :OUTC].astype(bf16)
    for copy in copies:
        copy.wait()


def body(staying_cache, leaving_cache, lengths, pairing, new_entries, queries, w_value, w_out):
    staying = jnp.swapaxes(staying_cache[0], 1, 2)
    leaving = jnp.swapaxes(leaving_cache[0], 1, 2)
    q = queries.reshape(REQ, STEPS * HEADS, WIDTH)

    first = pl.pallas_call(
        attend_kernel,
        out_shape=jax.ShapeDtypeStruct((MEMBERS, SENT, LANES), bf16),
        in_specs=[SMEM, VMEM, ANY, ANY, ANY, ANY],
        out_specs=ANY,
        scratch_shapes=[
            pltpu.VMEM((REQ, STEPS * HEADS, WIDTH), bf16),
            pltpu.VMEM((REQ, WIDTH, SLICE), bf16),
            pltpu.VMEM((REQ, WIDTH, SLICE), bf16),
            pltpu.VMEM((MEMBERS, VROWS, LANES), bf16),
            pltpu.VMEM((MEMBERS, SENT, LANES), bf16),
            pltpu.SemaphoreType.DMA((3, REQ)),
        ],
        name="attend",
    )(lengths, new_entries, q, staying, leaving, w_value)
    arrived = lax.all_to_all(first, "context", 0, 0)

    second = pl.pallas_call(
        merge_kernel,
        out_shape=jax.ShapeDtypeStruct((MEMBERS, CHUNK + ROWS, LANES), bf16),
        in_specs=[SMEM, VMEM],
        out_specs=VMEM,
        compiler_params=grant(4),
        name="merge",
    )(pairing, arrived)
    handed = lax.all_to_all(second, "context", 0, 0)

    forth, back, mine = pl.pallas_call(
        project_kernel,
        out_shape=(
            jax.ShapeDtypeStruct((FORTH_ROWS, LANES), bf16),
            jax.ShapeDtypeStruct((BACK_ROWS, LANES), bf16),
            jax.ShapeDtypeStruct((ROWS, LANES), f32),
        ),
        in_specs=[VMEM, VMEM],
        out_specs=(VMEM, VMEM, VMEM),
        compiler_params=grant(4),
        name="project",
    )(handed, w_out.T)

    up = [((t - 1) % TENSOR, t) for t in range(TENSOR)]
    down = [((t + 1) % TENSOR, t) for t in range(TENSOR)]
    from_left = lax.ppermute(forth, "tensor", up)
    from_right = lax.ppermute(back, "tensor", down)
    far_left = lax.ppermute(from_left[0 : FORTH_FAR + PART], "tensor", up)
    far_right = lax.ppermute(from_right[BACK_1:], "tensor", down)

    whole = jax.ShapeDtypeStruct((REQ, WIDTH, 2 * SLICE), bf16)
    cache = pl.pallas_call(
        keep_kernel,
        out_shape=whole,
        in_specs=[VMEM, VMEM],
        out_specs=ANY,
        scratch_shapes=[pltpu.SemaphoreType.DMA, pltpu.SemaphoreType.DMA((2, PIECES))],
        cost_estimate=pl.CostEstimate(flops=0, bytes_accessed=8_000_000, transcendentals=0),
        compiler_params=grant(1),
        name="keep",
    )(staying, forth)
    cache, near_total = pl.pallas_call(
        near_kernel,
        out_shape=(whole, jax.ShapeDtypeStruct((ROWS, LANES), f32)),
        in_specs=[ANY, VMEM, VMEM, VMEM],
        out_specs=(ANY, VMEM),
        scratch_shapes=[pltpu.SemaphoreType.DMA((4, PIECES))],
        input_output_aliases={0: 0},
        cost_estimate=pl.CostEstimate(flops=0, bytes_accessed=4_000_000, transcendentals=0),
        compiler_params=grant(1),
        name="near",
    )(cache, from_left, from_right, mine)
    cache, attn_out = pl.pallas_call(
        far_kernel,
        out_shape=(whole, jax.ShapeDtypeStruct((ROWS, OUTC), bf16)),
        in_specs=[ANY, VMEM, VMEM, VMEM],
        out_specs=(ANY, VMEM),
        scratch_shapes=[pltpu.SemaphoreType.DMA((2, PIECES))],
        input_output_aliases={0: 0},
        compiler_params=grant(1),
        name="far",
    )(cache, far_left, far_right, near_total)
    attn_out = attn_out.reshape(REQ, STEPS, OUTC)
    return (jnp.swapaxes(cache, 1, 2)[None], attn_out)


def solution(mesh):
    placed = (
        P("context", "dp", None, None),
        P("context", "dp", None, None),
        P("dp"),
        P("dp", None),
        P("dp", None, None),
        P("dp", None, "tensor", None),
        P("tensor", "context", None),
        P("tensor", "context"),
    )
    return jax.shard_map(
        body,
        mesh=mesh,
        in_specs=placed,
        out_specs=(P("context", "dp", None, None), P("dp", None, ("context", "tensor"))),
        check_vma=False,
    )
```

```python
import jax
import jax.numpy as jnp
from jax import lax
from jax.experimental import pallas as pl
from jax.experimental.pallas import tpu as pltpu
from jax.sharding import PartitionSpec as P

REQ = 4
STEPS = 2
HEADS = 16
LATENT = 512
WIDTH = 576
SLICE = 256
MEMBERS = 16
TENSOR = 4
LANES = 128
CHUNK = WIDTH * SLICE // (MEMBERS * LANES)
ROWS = REQ * STEPS
LTILES = LATENT // LANES
VROWS = LATENT // MEMBERS
STATS = LTILES * ROWS
CACHE = VROWS
PARTIAL = CACHE + CHUNK
SENT = PARTIAL + STATS + ROWS
EARLY = 96
OUTC = 112
PART = 2 * ROWS
PIECES = 2
PIECE = WIDTH // PIECES
FORTH_0 = 0
FORTH_FAR = WIDTH
FORTH_NEAR = FORTH_FAR + PART
FORTH_1 = FORTH_NEAR + PART
FORTH_ROWS = FORTH_1 + WIDTH
BACK_0 = PART
BACK_1 = BACK_0 + WIDTH
BACK_ROWS = BACK_1 + WIDTH

softmax_scale = 0.07216878364870322
large_negative = -1e30

f32 = jnp.float32
bf16 = jnp.bfloat16

VMEM = pl.BlockSpec(memory_space=pltpu.VMEM)
SMEM = pl.BlockSpec(memory_space=pltpu.SMEM)
ANY = pl.BlockSpec(memory_space=pl.ANY)


def grant(mib):
    return pltpu.CompilerParams(vmem_limit_bytes=mib * 2**20)


def nt_dot(a, b):
    return lax.dot_general(a, b, (((1,), (1,)), ((), ())), preferred_element_type=f32)


def attend_kernel(
    lengths_hbm,
    entries_hbm,
    queries_hbm,
    staying_hbm,
    leaving_hbm,
    w_value_hbm,
    out_hbm,
    lengths,
    entries,
    queries,
    staying,
    leaving,
    w_value,
    out,
    sems,
):
    member = lax.axis_index("context")
    tensor = lax.axis_index("tensor")
    kept_copies, moved_copies = [], []
    for b in range(REQ):
        moved_copies.append(
            pltpu.make_async_copy(leaving_hbm.at[b], leaving.at[b], sems.at[0, b])
        )
        moved_copies[b].start()
    length_copy = pltpu.make_async_copy(lengths_hbm, lengths, sems.at[3, 0])
    length_copy.start()
    entry_copy = pltpu.make_async_copy(entries_hbm, entries, sems.at[3, 1])
    entry_copy.start()
    query_copy = pltpu.make_async_copy(queries_hbm, queries, sems.at[2, 0])
    query_copy.start()
    value_copy = pltpu.make_async_copy(w_value_hbm, w_value, sems.at[2, 1])
    value_copy.start()
    for b in range(REQ):
        kept_copies.append(
            pltpu.make_async_copy(staying_hbm.at[b], staying.at[b], sems.at[1, b])
        )
        kept_copies[b].start()
    first_kept = member * SLICE
    first_moved = (MEMBERS + member) * SLICE
    row = lax.broadcasted_iota(jnp.int32, (STEPS * HEADS, SLICE), 0)
    slot = lax.broadcasted_iota(jnp.int32, (STEPS * HEADS, SLICE), 1)
    step = (row >= HEADS).astype(jnp.int32)
    lane = lax.broadcasted_iota(jnp.int32, (STEPS * HEADS, LANES), 1)
    parts = []
    length_copy.wait()
    entry_copy.wait()
    for b in range(REQ):
        moved_copies[b].wait()
        new_slot = lengths[b] - first_moved

        @pl.when((new_slot + STEPS > 0) & (new_slot < SLICE))
        def _():
            slots = lax.broadcasted_iota(jnp.int32, (STEPS, SLICE), 1)
            steps = lax.broadcasted_iota(jnp.int32, (STEPS, SLICE), 0)
            hit = (slots == new_slot + steps).astype(f32)
            placed = lax.dot_general(
                entries[b], hit.astype(bf16), (((0,), (0,)), ((), ())), preferred_element_type=f32
            )
            taken = jnp.max(hit, axis=0, keepdims=True) > 0.5
            leaving[b] = jnp.where(taken, placed, leaving[b].astype(f32)).astype(bf16)

    block = leaving[tensor]
    for c in range(MEMBERS):
        at, lanes = (c % 8) * CHUNK, (c // 8) * LANES
        out[c, CACHE : CACHE + CHUNK, :] = block[at : at + CHUNK, lanes : lanes + LANES]
    value_copy.wait()
    out[:, 0:VROWS, :] = w_value[...]
    early_copy = pltpu.make_async_copy(
        out.at[:, 0:EARLY, :], out_hbm.at[:, 0:EARLY, :], sems.at[2, 2]
    )
    early_copy.start()
    query_copy.wait()
    for b in range(REQ):
        kept_copies[b].wait()
        q = queries[b]
        limit = lengths[b] + 1 + step
        use_kept = slot + first_kept < limit
        use_moved = slot + first_moved < limit
        kept_scores = jnp.dot(q, staying[b], preferred_element_type=f32) * softmax_scale
        moved_scores = jnp.dot(q, leaving[b], preferred_element_type=f32) * softmax_scale
        kept_scores = jnp.where(use_kept, kept_scores, large_negative)
        moved_scores = jnp.where(use_moved, moved_scores, large_negative)
        peak = jnp.maximum(
            jnp.max(kept_scores, axis=1, keepdims=True),
            jnp.max(moved_scores, axis=1, keepdims=True),
        )
        peak = peak.astype(bf16).astype(f32)
        kept_w = jnp.where(use_kept, jnp.exp(kept_scores - peak), 0.0).astype(bf16)
        moved_w = jnp.where(use_moved, jnp.exp(moved_scores - peak), 0.0).astype(bf16)
        numerator = nt_dot(kept_w, staying[b, 0:LATENT, :]) + nt_dot(
            moved_w, leaving[b, 0:LATENT, :]
        )
        total = jnp.sum(kept_w.astype(f32) + moved_w.astype(f32), axis=1, keepdims=True)
        high = total.astype(bf16).astype(f32)
        stats = jnp.where(
            lane == 0, peak, jnp.where(lane == 1, high, jnp.where(lane == 2, total - high, 0.0))
        )
        both = jnp.concatenate([numerator, stats], axis=1)
        parts += [both[:HEADS], both[HEADS:]]
    by_head = jnp.transpose(jnp.stack(parts), (1, 0, 2))
    tiles = [by_head[:, :, i * LANES : (i + 1) * LANES] for i in range(LTILES + 1)]
    out[:, PARTIAL:SENT, :] = jnp.concatenate(tiles, axis=1).astype(bf16)
    late_copy = pltpu.make_async_copy(
        out.at[:, EARLY:SENT, :], out_hbm.at[:, EARLY:SENT, :], sems.at[2, 3]
    )
    late_copy.start()
    early_copy.wait()
    late_copy.wait()


def merge_kernel(pairing, arrived, out):
    offset = pairing[lax.axis_index("tensor"), 0]
    rows = arrived[:, PARTIAL:SENT, :].astype(f32)
    stats = rows[:, STATS:, :]
    peak = stats[:, :, 0:1]
    top = jnp.max(peak, axis=0, keepdims=True)
    factor = jnp.exp(peak - top)
    total = jnp.sum(factor * (stats[:, :, 1:2] + stats[:, :, 2:3]), axis=0)
    weights = arrived[:, 0:VROWS, :].reshape(LATENT, LANES)
    values = jnp.zeros((ROWS, LANES), f32)
    for i in range(LTILES):
        numerator = jnp.sum(factor * rows[:, ROWS * i : ROWS * (i + 1), :], axis=0)
        latent = (numerator / total).astype(bf16)
        values += jnp.dot(
            latent, weights[i * LANES : (i + 1) * LANES], preferred_element_type=f32
        )
    values = values.astype(bf16)
    for r in range(MEMBERS):
        source = lax.rem(r + MEMBERS - offset, MEMBERS)
        out[r, 0:CHUNK, :] = arrived[source, CACHE : CACHE + CHUNK, :]
        out[r, CHUNK : CHUNK + ROWS, :] = values


def project_kernel(handed, w_out, forth, back, mine):
    tensor = lax.axis_index("tensor")
    for c in range(MEMBERS):
        at = CHUNK * (c % 8)
        forth[(FORTH_0, FORTH_1)[c // 8] + at : (FORTH_0, FORTH_1)[c // 8] + at + CHUNK, :] = (
            handed[c, 0:CHUNK, :]
        )
        back[(BACK_0, BACK_1)[c // 8] + at : (BACK_0, BACK_1)[c // 8] + at + CHUNK, :] = (
            handed[c, 0:CHUNK, :]
        )
    flat = jnp.concatenate([handed[h, CHUNK : CHUNK + ROWS, :] for h in range(HEADS)], axis=1)
    columns = nt_dot(flat, w_out[...])
    pad = jnp.zeros((ROWS, LANES - OUTC), f32)
    parts = [
        jnp.concatenate([columns[:, OUTC * t : OUTC * (t + 1)], pad], axis=1)
        for t in range(TENSOR)
    ]

    def part_of(distance):
        target = lax.rem(tensor + distance, TENSOR)
        part = parts[0]
        for t in range(1, TENSOR):
            part = jnp.where(target == t, parts[t], part)
        return part

    def pieces(part):
        high = part.astype(bf16)
        return jnp.concatenate([high, (part - high.astype(f32)).astype(bf16)], axis=0)

    mine[...] = part_of(0)
    forth[FORTH_NEAR : FORTH_NEAR + PART, :] = pieces(part_of(1))
    forth[FORTH_FAR : FORTH_FAR + PART, :] = pieces(part_of(2))
    back[0:PART, :] = pieces(part_of(3))


def stores(block, first, cache, request, half, sems):
    lanes = SLICE + half * LANES
    return [
        pltpu.make_async_copy(
            block.at[first + PIECE * i : first + PIECE * (i + 1), :],
            cache.at[request, PIECE * i : PIECE * (i + 1), lanes : lanes + LANES],
            sems.at[i],
        )
        for i in range(PIECES)
    ]


def finish_all(copies):
    for copy in copies:
        copy.start()
    for copy in copies:
        copy.wait()


def keep_kernel(staying, forth, cache, sem, sems):
    tensor = lax.axis_index("tensor")
    finish_all(
        [pltpu.make_async_copy(staying, cache.at[:, :, 0:SLICE], sem)]
        + stores(forth, FORTH_0, cache, tensor, 0, sems.at[0])
        + stores(forth, FORTH_1, cache, tensor, 1, sems.at[1])
    )


def joined(pieces):
    pieces = pieces.astype(f32)
    return pieces[:ROWS] + pieces[ROWS:]


def near_kernel(cache_in, from_left, from_right, mine, cache, total, sems):
    tensor = lax.axis_index("tensor")
    left = lax.rem(tensor + TENSOR - 1, TENSOR)
    right = lax.rem(tensor + 1, TENSOR)
    total[...] = (
        mine[...]
        + joined(from_left[FORTH_NEAR : FORTH_NEAR + PART, :])
        + joined(from_right[0:PART, :])
    )
    finish_all(
        stores(from_left, FORTH_0, cache, left, 0, sems.at[0])
        + stores(from_left, FORTH_1, cache, left, 1, sems.at[1])
        + stores(from_right, BACK_0, cache, right, 0, sems.at[2])
        + stores(from_right, BACK_1, cache, right, 1, sems.at[3])
    )


def far_kernel(cache_in, far_left, far_right, near_total, cache, attn, sems):
    across = lax.rem(lax.axis_index("tensor") + 2, TENSOR)
    copies = stores(far_left, 0, cache, across, 0, sems.at[0])
    copies += stores(far_right, 0, cache, across, 1, sems.at[1])
    for copy in copies:
        copy.start()
    total = near_total[...] + joined(far_left[FORTH_FAR : FORTH_FAR + PART, :])
    attn[...] = total[:, :OUTC].astype(bf16)
    for copy in copies:
        copy.wait()


def body(staying_cache, leaving_cache, lengths, pairing, new_entries, queries, w_value, w_out):
    staying = jnp.swapaxes(staying_cache[0], 1, 2)
    leaving = jnp.swapaxes(leaving_cache[0], 1, 2)
    q = queries.reshape(REQ, STEPS * HEADS, WIDTH)

    first = pl.pallas_call(
        attend_kernel,
        out_shape=jax.ShapeDtypeStruct((MEMBERS, SENT, LANES), bf16),
        in_specs=[ANY] * 6,
        out_specs=ANY,
        scratch_shapes=[
            pltpu.SMEM((REQ,), jnp.int32),
            pltpu.VMEM((REQ, STEPS, WIDTH), bf16),
            pltpu.VMEM((REQ, STEPS * HEADS, WIDTH), bf16),
            pltpu.VMEM((REQ, WIDTH, SLICE), bf16),
            pltpu.VMEM((REQ, WIDTH, SLICE), bf16),
            pltpu.VMEM((MEMBERS, VROWS, LANES), bf16),
            pltpu.VMEM((MEMBERS, SENT, LANES), bf16),
            pltpu.SemaphoreType.DMA((4, REQ)),
        ],
        name="attend",
    )(lengths, new_entries, q, staying, leaving, w_value)
    arrived = lax.all_to_all(first, "context", 0, 0)

    second = pl.pallas_call(
        merge_kernel,
        out_shape=jax.ShapeDtypeStruct((MEMBERS, CHUNK + ROWS, LANES), bf16),
        in_specs=[SMEM, VMEM],
        out_specs=VMEM,
        compiler_params=grant(4),
        name="merge",
    )(pairing, arrived)
    handed = lax.all_to_all(second, "context", 0, 0)

    forth, back, mine = pl.pallas_call(
        project_kernel,
        out_shape=(
            jax.ShapeDtypeStruct((FORTH_ROWS, LANES), bf16),
            jax.ShapeDtypeStruct((BACK_ROWS, LANES), bf16),
            jax.ShapeDtypeStruct((ROWS, LANES), f32),
        ),
        in_specs=[VMEM, VMEM],
        out_specs=(VMEM, VMEM, VMEM),
        compiler_params=grant(4),
        name="project",
    )(handed, w_out.T)

    up = [((t - 1) % TENSOR, t) for t in range(TENSOR)]
    down = [((t + 1) % TENSOR, t) for t in range(TENSOR)]
    from_left = lax.ppermute(forth, "tensor", up)
    from_right = lax.ppermute(back, "tensor", down)
    far_left = lax.ppermute(from_left[0 : FORTH_FAR + PART], "tensor", up)
    far_right = lax.ppermute(from_right[BACK_1:], "tensor", down)

    whole = jax.ShapeDtypeStruct((REQ, WIDTH, 2 * SLICE), bf16)
    cache = pl.pallas_call(
        keep_kernel,
        out_shape=whole,
        in_specs=[VMEM, VMEM],
        out_specs=ANY,
        scratch_shapes=[pltpu.SemaphoreType.DMA, pltpu.SemaphoreType.DMA((2, PIECES))],
        cost_estimate=pl.CostEstimate(flops=0, bytes_accessed=8_000_000, transcendentals=0),
        compiler_params=grant(1),
        name="keep",
    )(staying, forth)
    cache, near_total = pl.pallas_call(
        near_kernel,
        out_shape=(whole, jax.ShapeDtypeStruct((ROWS, LANES), f32)),
        in_specs=[ANY, VMEM, VMEM, VMEM],
        out_specs=(ANY, VMEM),
        scratch_shapes=[pltpu.SemaphoreType.DMA((4, PIECES))],
        input_output_aliases={0: 0},
        cost_estimate=pl.CostEstimate(flops=0, bytes_accessed=4_000_000, transcendentals=0),
        compiler_params=grant(1),
        name="near",
    )(cache, from_left, from_right, mine)
    cache, attn_out = pl.pallas_call(
        far_kernel,
        out_shape=(whole, jax.ShapeDtypeStruct((ROWS, OUTC), bf16)),
        in_specs=[ANY, VMEM, VMEM, VMEM],
        out_specs=(ANY, VMEM),
        scratch_shapes=[pltpu.SemaphoreType.DMA((2, PIECES))],
        input_output_aliases={0: 0},
        compiler_params=grant(1),
        name="far",
    )(cache, far_left, far_right, near_total)
    attn_out = attn_out.reshape(REQ, STEPS, OUTC)
    return (jnp.swapaxes(cache, 1, 2)[None], attn_out)


def solution(mesh):
    placed = (
        P("context", "dp", None, None),
        P("context", "dp", None, None),
        P("dp"),
        P("dp", None),
        P("dp", None, None),
        P("dp", None, "tensor", None),
        P("tensor", "context", None),
        P("tensor", "context"),
    )
    return jax.shard_map(
        body,
        mesh=mesh,
        in_specs=placed,
        out_specs=(P("context", "dp", None, None), P("dp", None, ("context", "tensor"))),
        check_vma=False,
    )
```

```python
import jax
import jax.numpy as jnp
from jax import lax
from jax.experimental import pallas as pl
from jax.experimental.pallas import tpu as pltpu
from jax.sharding import PartitionSpec as P

REQ = 4
STEPS = 2
HEADS = 16
LATENT = 512
WIDTH = 576
SLICE = 256
MEMBERS = 16
TENSOR = 4
LANES = 128
CHUNK = WIDTH * SLICE // (MEMBERS * LANES)
ROWS = REQ * STEPS
LTILES = LATENT // LANES
VROWS = LATENT // MEMBERS
STATS = LTILES * ROWS
CACHE = VROWS
PARTIAL = CACHE + CHUNK
SENT = PARTIAL + STATS + ROWS
EARLY = 96
OUTC = 112
PART = 2 * ROWS
PIECES = 2
PIECE = WIDTH // PIECES
FORTH_FAR = 0
FORTH_0 = FORTH_FAR + PART
FORTH_1 = FORTH_0 + WIDTH
FORTH_NEAR = FORTH_1 + WIDTH
FORTH_ROWS = FORTH_NEAR + PART
BACK_0 = PART
BACK_1 = BACK_0 + WIDTH
BACK_ROWS = BACK_1 + WIDTH

softmax_scale = 0.07216878364870322
large_negative = -1e30

f32 = jnp.float32
bf16 = jnp.bfloat16

VMEM = pl.BlockSpec(memory_space=pltpu.VMEM)
SMEM = pl.BlockSpec(memory_space=pltpu.SMEM)
ANY = pl.BlockSpec(memory_space=pl.ANY)


def grant(mib):
    return pltpu.CompilerParams(vmem_limit_bytes=mib * 2**20)


def nt_dot(a, b):
    return lax.dot_general(a, b, (((1,), (1,)), ((), ())), preferred_element_type=f32)


def attend_kernel(
    lengths_hbm,
    entries_hbm,
    queries_hbm,
    staying_hbm,
    leaving_hbm,
    w_value_hbm,
    out_hbm,
    lengths,
    entries,
    queries,
    staying,
    leaving,
    w_value,
    out,
    sems,
):
    member = lax.axis_index("context")
    tensor = lax.axis_index("tensor")
    kept_copies, moved_copies = [], []
    for b in range(REQ):
        moved_copies.append(
            pltpu.make_async_copy(leaving_hbm.at[b], leaving.at[b], sems.at[0, b])
        )
        moved_copies[b].start()
    length_copy = pltpu.make_async_copy(lengths_hbm, lengths, sems.at[3, 0])
    length_copy.start()
    entry_copy = pltpu.make_async_copy(entries_hbm, entries, sems.at[3, 1])
    entry_copy.start()
    query_copy = pltpu.make_async_copy(queries_hbm, queries, sems.at[2, 0])
    query_copy.start()
    value_copy = pltpu.make_async_copy(w_value_hbm, w_value, sems.at[2, 1])
    value_copy.start()
    for b in range(REQ):
        kept_copies.append(
            pltpu.make_async_copy(staying_hbm.at[b], staying.at[b], sems.at[1, b])
        )
        kept_copies[b].start()
    first_kept = member * SLICE
    first_moved = (MEMBERS + member) * SLICE
    row = lax.broadcasted_iota(jnp.int32, (STEPS * HEADS, SLICE), 0)
    slot = lax.broadcasted_iota(jnp.int32, (STEPS * HEADS, SLICE), 1)
    step = (row >= HEADS).astype(jnp.int32)
    lane = lax.broadcasted_iota(jnp.int32, (STEPS * HEADS, LANES), 1)
    parts = []
    length_copy.wait()
    entry_copy.wait()
    for b in range(REQ):
        moved_copies[b].wait()
        new_slot = lengths[b] - first_moved

        @pl.when((new_slot + STEPS > 0) & (new_slot < SLICE))
        def _():
            slots = lax.broadcasted_iota(jnp.int32, (STEPS, SLICE), 1)
            steps = lax.broadcasted_iota(jnp.int32, (STEPS, SLICE), 0)
            hit = (slots == new_slot + steps).astype(f32)
            placed = lax.dot_general(
                entries[b], hit.astype(bf16), (((0,), (0,)), ((), ())), preferred_element_type=f32
            )
            taken = jnp.max(hit, axis=0, keepdims=True) > 0.5
            leaving[b] = jnp.where(taken, placed, leaving[b].astype(f32)).astype(bf16)

    block = leaving[tensor]
    for c in range(MEMBERS):
        at, lanes = (c % 8) * CHUNK, (c // 8) * LANES
        out[c, CACHE : CACHE + CHUNK, :] = block[at : at + CHUNK, lanes : lanes + LANES]
    value_copy.wait()
    out[:, 0:VROWS, :] = w_value[...]
    early_copy = pltpu.make_async_copy(
        out.at[:, 0:EARLY, :], out_hbm.at[:, 0:EARLY, :], sems.at[2, 2]
    )
    early_copy.start()
    query_copy.wait()
    for b in range(REQ):
        kept_copies[b].wait()
        q = queries[b]
        limit = lengths[b] + 1 + step
        use_kept = slot + first_kept < limit
        use_moved = slot + first_moved < limit
        kept_scores = jnp.dot(q, staying[b], preferred_element_type=f32) * softmax_scale
        moved_scores = jnp.dot(q, leaving[b], preferred_element_type=f32) * softmax_scale
        kept_scores = jnp.where(use_kept, kept_scores, large_negative)
        moved_scores = jnp.where(use_moved, moved_scores, large_negative)
        peak = jnp.maximum(
            jnp.max(kept_scores, axis=1, keepdims=True),
            jnp.max(moved_scores, axis=1, keepdims=True),
        )
        peak = peak.astype(bf16).astype(f32)
        kept_w = jnp.where(use_kept, jnp.exp(kept_scores - peak), 0.0).astype(bf16)
        moved_w = jnp.where(use_moved, jnp.exp(moved_scores - peak), 0.0).astype(bf16)
        numerator = nt_dot(kept_w, staying[b, 0:LATENT, :]) + nt_dot(
            moved_w, leaving[b, 0:LATENT, :]
        )
        total = jnp.sum(kept_w.astype(f32) + moved_w.astype(f32), axis=1, keepdims=True)
        high = total.astype(bf16).astype(f32)
        stats = jnp.where(
            lane == 0, peak, jnp.where(lane == 1, high, jnp.where(lane == 2, total - high, 0.0))
        )
        both = jnp.concatenate([numerator, stats], axis=1)
        parts += [both[:HEADS], both[HEADS:]]
    by_head = jnp.transpose(jnp.stack(parts), (1, 0, 2))
    tiles = [by_head[:, :, i * LANES : (i + 1) * LANES] for i in range(LTILES + 1)]
    out[:, PARTIAL:SENT, :] = jnp.concatenate(tiles, axis=1).astype(bf16)
    late_copy = pltpu.make_async_copy(
        out.at[:, EARLY:SENT, :], out_hbm.at[:, EARLY:SENT, :], sems.at[2, 3]
    )
    late_copy.start()
    early_copy.wait()
    late_copy.wait()


def merge_kernel(pairing, arrived, out):
    offset = pairing[lax.axis_index("tensor"), 0]
    rows = arrived[:, PARTIAL:SENT, :].astype(f32)
    stats = rows[:, STATS:, :]
    peak = stats[:, :, 0:1]
    top = jnp.max(peak, axis=0, keepdims=True)
    factor = jnp.exp(peak - top)
    total = jnp.sum(factor * (stats[:, :, 1:2] + stats[:, :, 2:3]), axis=0)
    weights = arrived[:, 0:VROWS, :].reshape(LATENT, LANES)
    values = jnp.zeros((ROWS, LANES), f32)
    for i in range(LTILES):
        numerator = jnp.sum(factor * rows[:, ROWS * i : ROWS * (i + 1), :], axis=0)
        latent = (numerator / total).astype(bf16)
        values += jnp.dot(
            latent, weights[i * LANES : (i + 1) * LANES], preferred_element_type=f32
        )
    values = values.astype(bf16)
    for r in range(MEMBERS):
        source = lax.rem(r + MEMBERS - offset, MEMBERS)
        out[r, 0:CHUNK, :] = arrived[source, CACHE : CACHE + CHUNK, :]
        out[r, CHUNK : CHUNK + ROWS, :] = values


def project_kernel(handed, w_out, forth, back, mine):
    tensor = lax.axis_index("tensor")
    for c in range(MEMBERS):
        at = CHUNK * (c % 8)
        forth[(FORTH_0, FORTH_1)[c // 8] + at : (FORTH_0, FORTH_1)[c // 8] + at + CHUNK, :] = (
            handed[c, 0:CHUNK, :]
        )
        back[(BACK_0, BACK_1)[c // 8] + at : (BACK_0, BACK_1)[c // 8] + at + CHUNK, :] = (
            handed[c, 0:CHUNK, :]
        )
    flat = jnp.concatenate([handed[h, CHUNK : CHUNK + ROWS, :] for h in range(HEADS)], axis=1)
    columns = nt_dot(flat, w_out[...])
    pad = jnp.zeros((ROWS, LANES - OUTC), f32)
    parts = [
        jnp.concatenate([columns[:, OUTC * t : OUTC * (t + 1)], pad], axis=1)
        for t in range(TENSOR)
    ]

    def part_of(distance):
        target = lax.rem(tensor + distance, TENSOR)
        part = parts[0]
        for t in range(1, TENSOR):
            part = jnp.where(target == t, parts[t], part)
        return part

    def pieces(part):
        high = part.astype(bf16)
        return jnp.concatenate([high, (part - high.astype(f32)).astype(bf16)], axis=0)

    mine[...] = part_of(0)
    forth[FORTH_NEAR : FORTH_NEAR + PART, :] = pieces(part_of(1))
    forth[FORTH_FAR : FORTH_FAR + PART, :] = pieces(part_of(2))
    back[0:PART, :] = pieces(part_of(3))


def stores(block, first, cache, request, half, sems, pieces=range(PIECES)):
    lanes = SLICE + half * LANES
    return [
        pltpu.make_async_copy(
            block.at[first + PIECE * i : first + PIECE * (i + 1), :],
            cache.at[request, PIECE * i : PIECE * (i + 1), lanes : lanes + LANES],
            sems.at[i],
        )
        for i in pieces
    ]


def finish_all(copies):
    for copy in copies:
        copy.start()
    for copy in copies:
        copy.wait()


def keep_kernel(staying, forth, cache, sem, sems):
    tensor = lax.axis_index("tensor")
    finish_all(
        [pltpu.make_async_copy(staying, cache.at[:, :, 0:SLICE], sem)]
        + stores(forth, FORTH_0, cache, tensor, 0, sems.at[0])
        + stores(forth, FORTH_1, cache, tensor, 1, sems.at[1])
    )


def joined(pieces):
    pieces = pieces.astype(f32)
    return pieces[:ROWS] + pieces[ROWS:]


def near_kernel(cache_in, from_left, from_right, mine, cache, total, sems):
    tensor = lax.axis_index("tensor")
    left = lax.rem(tensor + TENSOR - 1, TENSOR)
    right = lax.rem(tensor + 1, TENSOR)
    total[...] = (
        mine[...]
        + joined(from_left[FORTH_NEAR : FORTH_NEAR + PART, :])
        + joined(from_right[0:PART, :])
    )
    finish_all(
        stores(from_left, FORTH_0, cache, left, 0, sems.at[0])
        + stores(from_left, FORTH_1, cache, left, 1, sems.at[1])
        + stores(from_right, BACK_0, cache, right, 0, sems.at[2])
        + stores(from_right, BACK_1, cache, right, 1, sems.at[3])
    )


def far_kernel(cache_in, far_left, far_right, near_total, cache, attn, sems):
    across = lax.rem(lax.axis_index("tensor") + 2, TENSOR)
    copies = stores(far_left, FORTH_0, cache, across, 0, sems.at[0])
    copies += stores(far_left, FORTH_1, cache, across, 1, sems.at[1], [0])
    copies += stores(far_right, -PIECE, cache, across, 1, sems.at[1], [1])
    for copy in copies:
        copy.start()
    total = near_total[...] + joined(far_left[FORTH_FAR : FORTH_FAR + PART, :])
    attn[...] = total[:, :OUTC].astype(bf16)
    for copy in copies:
        copy.wait()


def body(staying_cache, leaving_cache, lengths, pairing, new_entries, queries, w_value, w_out):
    staying = jnp.swapaxes(staying_cache[0], 1, 2)
    leaving = jnp.swapaxes(leaving_cache[0], 1, 2)
    q = queries.reshape(REQ, STEPS * HEADS, WIDTH)

    first = pl.pallas_call(
        attend_kernel,
        out_shape=jax.ShapeDtypeStruct((MEMBERS, SENT, LANES), bf16),
        in_specs=[ANY] * 6,
        out_specs=ANY,
        scratch_shapes=[
            pltpu.SMEM((REQ,), jnp.int32),
            pltpu.VMEM((REQ, STEPS, WIDTH), bf16),
            pltpu.VMEM((REQ, STEPS * HEADS, WIDTH), bf16),
            pltpu.VMEM((REQ, WIDTH, SLICE), bf16),
            pltpu.VMEM((REQ, WIDTH, SLICE), bf16),
            pltpu.VMEM((MEMBERS, VROWS, LANES), bf16),
            pltpu.VMEM((MEMBERS, SENT, LANES), bf16),
            pltpu.SemaphoreType.DMA((4, REQ)),
        ],
        name="attend",
    )(lengths, new_entries, q, staying, leaving, w_value)
    arrived = lax.all_to_all(first, "context", 0, 0)

    second = pl.pallas_call(
        merge_kernel,
        out_shape=jax.ShapeDtypeStruct((MEMBERS, CHUNK + ROWS, LANES), bf16),
        in_specs=[SMEM, VMEM],
        out_specs=VMEM,
        compiler_params=grant(4),
        name="merge",
    )(pairing, arrived)
    handed = lax.all_to_all(second, "context", 0, 0)

    forth, back, mine = pl.pallas_call(
        project_kernel,
        out_shape=(
            jax.ShapeDtypeStruct((FORTH_ROWS, LANES), bf16),
            jax.ShapeDtypeStruct((BACK_ROWS, LANES), bf16),
            jax.ShapeDtypeStruct((ROWS, LANES), f32),
        ),
        in_specs=[VMEM, VMEM],
        out_specs=(VMEM, VMEM, VMEM),
        compiler_params=grant(4),
        name="project",
    )(handed, w_out.T)

    up = [((t - 1) % TENSOR, t) for t in range(TENSOR)]
    down = [((t + 1) % TENSOR, t) for t in range(TENSOR)]
    from_left = lax.ppermute(forth, "tensor", up)
    from_right = lax.ppermute(back, "tensor", down)
    far_left = lax.ppermute(from_left[0 : FORTH_1 + PIECE], "tensor", up)
    far_right = lax.ppermute(from_right[BACK_1 + PIECE :], "tensor", down)

    whole = jax.ShapeDtypeStruct((REQ, WIDTH, 2 * SLICE), bf16)
    cache = pl.pallas_call(
        keep_kernel,
        out_shape=whole,
        in_specs=[VMEM, VMEM],
        out_specs=ANY,
        scratch_shapes=[pltpu.SemaphoreType.DMA, pltpu.SemaphoreType.DMA((2, PIECES))],
        cost_estimate=pl.CostEstimate(flops=0, bytes_accessed=8_000_000, transcendentals=0),
        compiler_params=grant(1),
        name="keep",
    )(staying, forth)
    cache, near_total = pl.pallas_call(
        near_kernel,
        out_shape=(whole, jax.ShapeDtypeStruct((ROWS, LANES), f32)),
        in_specs=[ANY, VMEM, VMEM, VMEM],
        out_specs=(ANY, VMEM),
        scratch_shapes=[pltpu.SemaphoreType.DMA((4, PIECES))],
        input_output_aliases={0: 0},
        cost_estimate=pl.CostEstimate(flops=0, bytes_accessed=4_000_000, transcendentals=0),
        compiler_params=grant(1),
        name="near",
    )(cache, from_left, from_right, mine)
    cache, attn_out = pl.pallas_call(
        far_kernel,
        out_shape=(whole, jax.ShapeDtypeStruct((ROWS, OUTC), bf16)),
        in_specs=[ANY, VMEM, VMEM, VMEM],
        out_specs=(ANY, VMEM),
        scratch_shapes=[pltpu.SemaphoreType.DMA((2, PIECES))],
        input_output_aliases={0: 0},
        compiler_params=grant(1),
        name="far",
    )(cache, far_left, far_right, near_total)
    attn_out = attn_out.reshape(REQ, STEPS, OUTC)
    return (jnp.swapaxes(cache, 1, 2)[None], attn_out)


def solution(mesh):
    placed = (
        P("context", "dp", None, None),
        P("context", "dp", None, None),
        P("dp"),
        P("dp", None),
        P("dp", None, None),
        P("dp", None, "tensor", None),
        P("tensor", "context", None),
        P("tensor", "context"),
    )
    return jax.shard_map(
        body,
        mesh=mesh,
        in_specs=placed,
        out_specs=(P("context", "dp", None, None), P("dp", None, ("context", "tensor"))),
        check_vma=False,
    )
```
